256 devices in a mesh: row: 8 (over x, core), col: 32 (over y, z).
Axes of the slice: x: 4, y: 4, z: 8, core: 2. Of those that a mesh axis runs over, the one named last changes fastest.
Arguments:
- source: bfloat16 [32768, 64], P(('row', 'col')), may hold values from -3 to 3
- target: bfloat16 [131072, 64], P(('col', 'row')), may hold values from -3 to 3
- log_a: float32 [32768], P('row'), may hold values from -1 to 1
- log_b: float32 [131072], P('col'), may hold values from -1 to 1
- start_potential: float32 [131072], P(('col', 'row')), may hold values from -8 to 300
Outputs:
- source_potential: float32 [32768], P(('row', 'col'))
- target_potential: float32 [131072], P(('col', 'row'))
The draws below stay inside these ranges and needn't reach their ends.
All inputs are finite; a program needn't handle non-finite values.
Results may differ from the reference program's by a relative error of at most 0.0003.
Values may be sent and summed in bfloat16 or wider, within the bound.
No kernel may reach another device: no remote copies, remote signals or barrier semaphores. Data moves between devices by JAX's collectives and lax.ppermute only.
A program may use at most 64 MiB of HBM per device.

```python
import jax
import jax.numpy as jnp
from jax import lax

FEAT = 64
N_SRC = 32768
N_TGT = 131072


def draw_start_potential(key, part):
    key = jax.random.fold_in(key, 7)
    return jnp.clip(2.0 * jax.random.normal(key, (N_TGT,), jnp.float32), -8.0, 8.0)


def levels(key, extent, shards, smallest, top_value):
    level, own = 1.0, jax.random.fold_in(key, 6)
    for dim, shards_of in shards:
        draws = jnp.exp(jax.random.uniform(jax.random.fold_in(own, dim), (shards_of,), jnp.float32, smallest / len(shards), top_value / len(shards)))
        level = level * jnp.repeat(draws, extent[dim] // shards_of).reshape([-1 if axis == dim else 1 for axis in range(len(extent))])
    return level


def scatter_about(own_key, dims, scale, limit, shards=(), dtype=jnp.bfloat16):
    result = scale * jax.random.normal(own_key, dims, jnp.float32)
    if shards:
        result = result * levels(own_key, dims, shards, -0.22, 0.18)
    return jnp.clip(result, -limit, limit).astype(dtype)


def setup_inputs(seed: int = 0) -> dict:
    arg_keys = jax.random.split(jax.random.key(seed), 6)
    source = scatter_about(arg_keys[0], (N_SRC, FEAT), 0.5, 3.0, ((0, 256),))
    target = scatter_about(arg_keys[1], (N_TGT, FEAT), 0.5, 3.0, ((0, 256),))
    log_a = jnp.clip(jax.random.uniform(arg_keys[2], (N_SRC,), jnp.float32, -1.0, 1.0) * levels(arg_keys[2], (N_SRC,), ((0, 8),), -0.4, 0.0), -1.0, 1.0)
    log_b = jnp.clip(jax.random.uniform(arg_keys[3], (N_TGT,), jnp.float32, -1.0, 1.0) * levels(arg_keys[3], (N_TGT,), ((0, 32),), -0.4, 0.0), -1.0, 1.0)
    start_potential = draw_start_potential(jax.random.fold_in(arg_keys[5], 71), 0)
    return dict(source=source, target=target, log_a=log_a, log_b=log_b, start_potential=start_potential)


def cost_tile(block, target, sq_y):
    dots = jnp.dot(block, target.T, preferred_element_type=jnp.float32)
    wide = block.astype(jnp.float32)
    sq_x = jnp.sum(wide * wide, axis=1)
    return 0.5 * sq_x[:, None] + 0.5 * sq_y[None, :] - dots


def reference(source, target, log_a, log_b, start_potential):
    wide = target.astype(jnp.float32)
    sq_y = jnp.sum(wide * wide, axis=1)
    rows = min(256, N_SRC)
    count = N_SRC // rows
    blocks = source.reshape(count, rows, FEAT)
    masses = log_a.reshape(count, rows)

    def advance(carry, inputs):
        col_max, col_sum = carry
        block, mass = inputs
        cost = cost_tile(block, target, sq_y)
        scores = start_potential[None, :] - cost
        peak = jnp.max(scores, axis=1)
        total = jnp.sum(jnp.exp(scores - peak[:, None]), axis=1)
        fresh = mass - (peak + jnp.log(total))
        backward = fresh[:, None] - cost
        block_max = jnp.max(backward, axis=0)
        new_max = jnp.maximum(col_max, block_max)
        new_sum = col_sum * jnp.exp(col_max - new_max) + jnp.sum(jnp.exp(backward - new_max[None, :]), axis=0)
        return (new_max, new_sum), fresh

    start = (jnp.full((N_TGT,), -1e30, jnp.float32), jnp.zeros((N_TGT,), jnp.float32))
    (col_max, col_sum), fresh = lax.scan(advance, start, (blocks, masses))
    source_potential = fresh.reshape(N_SRC)
    target_potential = log_b - (col_max + jnp.log(col_sum))
    return source_potential, target_potential
```

```python
import functools

import jax
import jax.numpy as jnp
from jax import lax
from jax.experimental import pallas as pl
from jax.experimental.pallas import tpu as pltpu
from jax.sharding import PartitionSpec as P

F32 = jnp.float32
BF16 = jnp.bfloat16
LANES = 128
PACKED = 256
PIECE = PACKED + 16
LOW, HIGH = 1e-24, 1e36


def params(mib=36):
    return pltpu.CompilerParams(vmem_limit_bytes=mib * 2**20)


def lanes_to_rows(values):
    return jnp.broadcast_to(values, (LANES, LANES)).T


def times(left, right):
    return lax.dot_general(left, right, (((1,), (1,)), ((), ())), preferred_element_type=F32)


def wide(rows, columns):
    return jnp.concatenate([rows] * (columns // LANES), axis=1)


def fold(values, combine):
    rows, columns = values.shape
    return combine(values.reshape(rows // 8, 8, columns), axis=0)


def prepare_kernel(x_ref, y_ref, g_ref, xs_ref, ys_ref, sqx_ref, sqy_ref, part_ref):
    half = x_ref.shape[0] // 2
    x = x_ref[...]
    packed = jnp.concatenate([x[:half], x[half:]], axis=1)
    for peer in range(xs_ref.shape[0]):
        xs_ref[peer] = packed
    xt = x.astype(F32).T
    sqx_ref[...] = jnp.sum(xt * xt, axis=0, keepdims=True)
    y = y_ref[...]
    ys_ref[pl.ds(0, PACKED), :] = jnp.concatenate([y[:PACKED], y[PACKED:]], axis=1)
    yt = y.astype(F32).T
    sqy = jnp.sum(yt * yt, axis=0, keepdims=True)
    part_ref[...] = jnp.zeros_like(part_ref)
    for k in range(4):
        own = sqy[:, k * LANES : (k + 1) * LANES]
        sqy_ref[pl.ds(k, 1), :] = own
        rest = g_ref[pl.ds(k, 1), :] - 0.5 * own
        for level in range(3):
            part = rest.astype(BF16).astype(F32)
            part_ref[pl.ds(4 * level + k, 1), :] = part
            rest = rest - part
    ys_ref[pl.ds(PACKED, 16), :] = part_ref[...].astype(BF16)


def prepare(source, target, g, peers):
    return pl.pallas_call(
        prepare_kernel,
        out_shape=(
            jax.ShapeDtypeStruct((peers, 64, LANES), BF16),
            jax.ShapeDtypeStruct((PIECE, LANES), BF16),
            jax.ShapeDtypeStruct((1, LANES), F32),
            jax.ShapeDtypeStruct((4, LANES), F32),
        ),
        scratch_shapes=[pltpu.VMEM((16, LANES), F32)],
        name="prepare",
        compiler_params=params(),
    )(source, target, g.reshape(4, LANES))


def pieces_of(refs):
    return [ref.at[k] for ref in refs for k in range(ref.shape[0])]


def spread(xs_ref, x1, x2):
    zeros = jnp.zeros((64, 64), BF16)
    for q in range(xs_ref.shape[0]):
        both = xs_ref[q]
        top, low = both[:, :64], both[:, 64:]
        x1[pl.ds(q * 128, 64), :] = jnp.concatenate([top, zeros], axis=1)
        x1[pl.ds(q * 128 + 64, 64), :] = jnp.concatenate([low, zeros], axis=1)
        x2[pl.ds(q * 128, 64), :] = jnp.concatenate([zeros, top], axis=1)
        x2[pl.ds(q * 128 + 64, 64), :] = jnp.concatenate([zeros, low], axis=1)


def row_kernel(xs_ref, *refs, groups):
    y_refs, (lp_ref, x1, x2, h1, h2) = refs[:groups], refs[groups:]
    ys = pieces_of(y_refs)
    rows = x1.shape[0]
    tile = 1024
    spread(xs_ref, x1, x2)
    terms = []
    for y in ys:
        parts = y[pl.ds(PACKED, 16), :].astype(F32)
        terms.append(parts[0:4] + parts[4:8] + parts[8:12])
    shift = jnp.max(functools.reduce(jnp.maximum, terms))
    for p, term in enumerate(terms):
        term = term - shift
        for k in range(2):
            at = pl.ds(p * PACKED + k * LANES, LANES)
            h1[at, :] = lanes_to_rows(term[k : k + 1])
            h2[at, :] = lanes_to_rows(term[k + 2 : k + 3])

    def scores(p, x, h, n, columns):
        z = times(ys[p][pl.ds(0, PACKED), :], x[pl.ds(n * columns, columns), :])
        return z + wide(h[pl.ds(p * PACKED, PACKED), :], columns)

    def total(n, seen):
        acc = jnp.zeros((8, tile), F32)
        for p in range(len(ys)):
            for x, h in ((x1, h1), (x2, h2)):
                acc += fold(jnp.exp(scores(p, x, h, n, tile)), jnp.sum)
        total = jnp.sum(acc, axis=0, keepdims=True)
        lp = shift + jnp.log(total)
        for k in range(tile // LANES):
            lp_ref[pl.ds(n * (tile // LANES) + k, 1), :] = lp[:, k * LANES : (k + 1) * LANES]
        return jnp.minimum(seen[0], jnp.min(total)), jnp.maximum(seen[1], jnp.max(total))

    least, most = lax.fori_loop(0, rows // tile, total, (jnp.float32(1.0), jnp.float32(1.0)))

    @pl.when(jnp.logical_not((least > LOW) & (most < HIGH)))
    def _():
        def exact(n, carry):
            peak = jnp.full((8, LANES), -1e30, F32)
            for p in range(len(ys)):
                for x, h in ((x1, h1), (x2, h2)):
                    peak = jnp.maximum(peak, fold(scores(p, x, h, n, LANES), jnp.max))
            peak = jnp.max(peak, axis=0, keepdims=True)
            acc = jnp.zeros((8, LANES), F32)
            for p in range(len(ys)):
                for x, h in ((x1, h1), (x2, h2)):
                    acc += fold(jnp.exp(scores(p, x, h, n, LANES) - peak), jnp.sum)
            total = jnp.sum(acc, axis=0, keepdims=True)
            lp_ref[pl.ds(n, 1), :] = shift + peak + jnp.log(total)
            return carry

        lax.fori_loop(0, rows // LANES, exact, 0)


def row_pass(xs, ys):
    peers = xs.shape[0]
    rows = peers * 128
    packed = sum(y.shape[0] for y in ys) * PACKED
    return pl.pallas_call(
        functools.partial(row_kernel, groups=len(ys)),
        out_shape=jax.ShapeDtypeStruct((peers, LANES), F32),
        scratch_shapes=[
            pltpu.VMEM((rows, LANES), BF16),
            pltpu.VMEM((rows, LANES), BF16),
            pltpu.VMEM((packed, LANES), F32),
            pltpu.VMEM((packed, LANES), F32),
        ],
        name="row_pass",
        compiler_params=params(),
        cost_estimate=pl.CostEstimate(
            flops=4 * rows * packed * 128, bytes_accessed=4 * 2**20, transcendentals=2 * rows * packed
        ),
    )(xs, *ys)


def log_sum(parts):
    peak = jnp.max(parts, axis=0)
    return peak + jnp.log(jnp.sum(jnp.exp(parts - peak[None]), axis=0))


def column_kernel(xs_ref, lp_ref, log_a_ref, *refs, groups):
    y_refs, (r_ref, lt_ref, x1, x2, rows_ref) = refs[:groups], refs[groups:]
    ys = pieces_of(y_refs)
    rows = x1.shape[0]
    spread(xs_ref, x1, x2)
    r = log_a_ref[...] - log_sum(lp_ref[...])
    r_ref[...] = r
    shift = jnp.max(r)
    for k in range(rows // LANES):
        rows_ref[pl.ds(k * LANES, LANES), :] = lanes_to_rows(r[k : k + 1] - shift)
    chunk = 512

    def scores(x, m, y, chunk):
        at = pl.ds(m * chunk, chunk)
        z = times(x[at, :], y)
        return z + wide(rows_ref[at, :], y.shape[0])

    least, most = jnp.float32(1.0), jnp.float32(1.0)
    for first in range(0, len(ys), 4):
        y = jnp.concatenate([ys[first + k][pl.ds(0, PACKED), :] for k in range(4)], axis=0)
        for side, x in enumerate((x1, x2)):
            acc = jnp.zeros((8, 4 * PACKED), F32)
            for m in range(rows // chunk):
                acc += fold(jnp.exp(scores(x, m, y, chunk)), jnp.sum)
            total = jnp.sum(acc, axis=0, keepdims=True)
            lt = shift + jnp.log(total)
            for k in range(4):
                lt_ref[first + k, pl.ds(side, 1), :] = lt[:, k * PACKED : (k + 1) * PACKED]
            least = jnp.minimum(least, jnp.min(total))
            most = jnp.maximum(most, jnp.max(total))

    @pl.when(jnp.logical_not((least > LOW) & (most < HIGH)))
    def _():
        for p in range(len(ys)):
            y = ys[p][pl.ds(0, PACKED), :]
            for side, x in enumerate((x1, x2)):

                def top(m, peak):
                    return jnp.maximum(peak, fold(scores(x, m, y, 256), jnp.max))

                peak = lax.fori_loop(0, rows // 256, top, jnp.full((8, PACKED), -1e30, F32))
                peak = jnp.max(peak, axis=0, keepdims=True)

                def add(m, acc):
                    return acc + fold(jnp.exp(scores(x, m, y, 256) - peak), jnp.sum)

                acc = lax.fori_loop(0, rows // 256, add, jnp.zeros((8, PACKED), F32))
                total = jnp.sum(acc, axis=0, keepdims=True)
                lt_ref[p, pl.ds(side, 1), :] = shift + peak + jnp.log(total)


def column_pass(xs, lps, log_a, ys):
    peers = xs.shape[0]
    rows = peers * 128
    count = sum(y.shape[0] for y in ys)
    return pl.pallas_call(
        functools.partial(column_kernel, groups=len(ys)),
        out_shape=(
            jax.ShapeDtypeStruct((peers, LANES), F32),
            jax.ShapeDtypeStruct((count, 2, PACKED), F32),
        ),
        scratch_shapes=[
            pltpu.VMEM((rows, LANES), BF16),
            pltpu.VMEM((rows, LANES), BF16),
            pltpu.VMEM((rows, LANES), F32),
        ],
        name="column_pass",
        compiler_params=params(),
        cost_estimate=pl.CostEstimate(
            flops=4 * rows * count * PACKED * 128,
            bytes_accessed=4 * 2**20,
            transcendentals=2 * rows * count * PACKED,
        ),
    )(xs, lps, log_a, *ys)


def finish_kernel(lt_ref, r_ref, log_b_ref, sqx_ref, sqy_ref, at_ref, f_ref, g_ref):
    f_ref[...] = r_ref[pl.ds(at_ref[0], 1), :] + 0.5 * sqx_ref[...]
    g_ref[...] = log_b_ref[at_ref[1]] + 0.5 * sqy_ref[...] - log_sum(lt_ref[...])


def finish(lt, r, log_b, sqx, sqy, at):
    vmem = pl.BlockSpec(memory_space=pltpu.VMEM)
    return pl.pallas_call(
        finish_kernel,
        in_specs=[vmem] * 5 + [pl.BlockSpec(memory_space=pltpu.SMEM)],
        out_shape=(
            jax.ShapeDtypeStruct((1, LANES), F32),
            jax.ShapeDtypeStruct((4, LANES), F32),
        ),
        name="finish",
        compiler_params=params(),
    )(lt, r, log_b, sqx, sqy, at)


def exchange(values, axis, groups=None):
    return lax.all_to_all(values, axis, 0, 0, tiled=True, axis_index_groups=groups)


def to_all(values, axis, peers, groups=None):
    return exchange(jnp.broadcast_to(values[None], (peers,) + values.shape), axis, groups)


def per_device(source, target, log_a, log_b, start_potential):
    rows, cols = lax.axis_size("row"), lax.axis_size("col")
    row, col = lax.axis_index("row"), lax.axis_index("col")
    chips = rows // 2
    xs, ys, sqx, sqy = prepare(source, target, start_potential, cols)

    def along(step):
        pairs = [(2 * x + c, 2 * ((x + step) % chips) + c) for x in range(chips) for c in range(2)]
        return lax.ppermute(ys, "row", pairs)

    same = jnp.stack([ys] + [along(step) for step in range(1, chips)])
    other = lax.ppermute(same, "row", [(i, i ^ 1) for i in range(rows)])
    xs = exchange(xs, "col")

    lp = row_pass(xs, [same, other])
    lps = to_all(lp, "col", cols).reshape(cols, cols, LANES)
    r, lt = column_pass(xs, lps, log_a.reshape(cols, LANES), [same, other])

    chip, core = row // 2, row % 2
    owner = jnp.arange(rows)
    piece = (chip - owner // 2) % chips + chips * ((owner % 2) ^ core)
    lt = jnp.take(lt.reshape(rows, 4, LANES), piece, axis=0)
    lt = exchange(lt, "row")
    f, g = finish(lt, r, log_b.reshape(rows, 4, LANES), sqx, sqy, jnp.stack([col, row]))
    return f.reshape(LANES), g.reshape(4 * LANES)


def solution(mesh):
    placed = (
        P(("row", "col"), None),
        P(("col", "row"), None),
        P("row"),
        P("col"),
        P(("col", "row")),
    )
    return jax.shard_map(
        per_device,
        mesh=mesh,
        in_specs=placed,
        out_specs=(P(("row", "col")), P(("col", "row"))),
        check_vma=False,
    )
```

```python
import functools

import jax
import jax.numpy as jnp
from jax import lax
from jax.experimental import pallas as pl
from jax.experimental.pallas import tpu as pltpu
from jax.sharding import PartitionSpec as P

F32 = jnp.float32
BF16 = jnp.bfloat16
LANES = 128
PACKED = 256
PIECE = PACKED + 16
LOW, HIGH = 1e-24, 1e36


def params(mib=16):
    return pltpu.CompilerParams(vmem_limit_bytes=mib * 2**20)


def lanes_to_rows(values):
    return jnp.broadcast_to(values, (LANES, LANES)).T


def times(left, right):
    return lax.dot_general(left, right, (((1,), (1,)), ((), ())), preferred_element_type=F32)


def wide(rows, columns):
    return jnp.concatenate([rows] * (columns // LANES), axis=1)


def fold(values, combine):
    rows, columns = values.shape
    return combine(values.reshape(rows // 8, 8, columns), axis=0)


def prepare_kernel(
    xt_hbm, yt_hbm, g_hbm, xs_ref, ys_ref, sqx_ref, sqy_ref, part_ref, xt_ref, yt_ref, g_ref, sems
):
    copies = [
        pltpu.make_async_copy(src, dst, sems.at[k])
        for k, (src, dst) in enumerate(((xt_hbm, xt_ref), (yt_hbm, yt_ref), (g_hbm, g_ref)))
    ]
    for copy in copies:
        copy.start()
    for copy in copies:
        copy.wait()
    xt = xt_ref[...].astype(F32)
    x = xt.T.astype(BF16)
    xs_ref[...] = jnp.concatenate([x[:64], x[64:]], axis=1)
    sqx_ref[...] = jnp.sum(xt * xt, axis=0, keepdims=True)
    yt = yt_ref[...].astype(F32)
    y = yt.T.astype(BF16)
    ys_ref[pl.ds(0, PACKED), :] = jnp.concatenate([y[:PACKED], y[PACKED:]], axis=1)
    sqy = jnp.sum(yt * yt, axis=0, keepdims=True)
    part_ref[...] = jnp.zeros_like(part_ref)
    for k in range(4):
        own = sqy[:, k * LANES : (k + 1) * LANES]
        sqy_ref[pl.ds(k, 1), :] = own
        rest = g_ref[pl.ds(k, 1), :] - 0.5 * own
        for level in range(3):
            part = rest.astype(BF16).astype(F32)
            part_ref[pl.ds(4 * level + k, 1), :] = part
            rest = rest - part
    ys_ref[pl.ds(PACKED, 16), :] = part_ref[...].astype(BF16)


def prepare(source, target, g):
    return pl.pallas_call(
        prepare_kernel,
        out_shape=(
            jax.ShapeDtypeStruct((64, LANES), BF16),
            jax.ShapeDtypeStruct((PIECE, LANES), BF16),
            jax.ShapeDtypeStruct((1, LANES), F32),
            jax.ShapeDtypeStruct((4, LANES), F32),
        ),
        in_specs=[pl.BlockSpec(memory_space=pltpu.MemorySpace.HBM)] * 3,
        scratch_shapes=[
            pltpu.VMEM((16, LANES), F32),
            pltpu.VMEM(source.shape[::-1], BF16),
            pltpu.VMEM(target.shape[::-1], BF16),
            pltpu.VMEM((4, LANES), F32),
            pltpu.SemaphoreType.DMA((3,)),
        ],
        name="prepare",
        compiler_params=params(60),
    )(source.T, target.T, g.reshape(4, LANES))


def pair_kernel(xs_ref, far_ref, both_ref):
    peers = both_ref.shape[0]
    second = lax.axis_index("col") // (2 * peers)
    for peer in range(peers):
        both_ref[peer, second] = xs_ref[...]
        both_ref[peer, 1 - second] = far_ref[...]


def pair(xs, far, peers):
    return pl.pallas_call(
        pair_kernel,
        out_shape=jax.ShapeDtypeStruct((peers, 2) + xs.shape, BF16),
        name="pair",
        compiler_params=params(),
    )(xs, far)


def spread(xs_ref, x1, x2):
    zeros = jnp.zeros((64, 64), BF16)
    peers = xs_ref.shape[0]
    for q in range(2 * peers):
        both = xs_ref[q % peers, q // peers]
        top, low = both[:, :64], both[:, 64:]
        x1[pl.ds(q * 128, 64), :] = jnp.concatenate([top, zeros], axis=1)
        x1[pl.ds(q * 128 + 64, 64), :] = jnp.concatenate([low, zeros], axis=1)
        x2[pl.ds(q * 128, 64), :] = jnp.concatenate([zeros, top], axis=1)
        x2[pl.ds(q * 128 + 64, 64), :] = jnp.concatenate([zeros, low], axis=1)


def pieces_of(refs):
    return [ref.at[k] for ref in refs for k in range(ref.shape[0])]


def row_sums(x1, x2, y_refs, h1, h2, put):
    ys = pieces_of(y_refs)
    rows = x1.shape[0]
    tile = 1024
    terms = []
    for y in ys:
        parts = y[pl.ds(PACKED, 16), :].astype(F32)
        terms.append(parts[0:4] + parts[4:8] + parts[8:12])
    shift = jnp.max(functools.reduce(jnp.maximum, terms))

    def scores(p, x, h, n, columns):
        z = times(ys[p][pl.ds(0, PACKED), :], x[pl.ds(n * columns, columns), :])
        return z + wide(h[pl.ds(p * PACKED, PACKED), :], columns)

    least, most = jnp.float32(1.0), jnp.float32(1.0)
    for n in range(rows // tile):
        acc = jnp.zeros((8, tile), F32)
        for p in range(len(ys)):
            if n == 0:
                term = terms[p] - shift
                for k in range(2):
                    at = pl.ds(p * PACKED + k * LANES, LANES)
                    h1[at, :] = lanes_to_rows(term[k : k + 1])
                    h2[at, :] = lanes_to_rows(term[k + 2 : k + 3])
            for x, h in ((x1, h1), (x2, h2)):
                acc += fold(jnp.exp(scores(p, x, h, n, tile)), jnp.sum)
        total = jnp.sum(acc, axis=0, keepdims=True)
        lp = shift + jnp.log(total)
        for k in range(tile // LANES):
            put(n * (tile // LANES) + k, lp[:, k * LANES : (k + 1) * LANES])
        least = jnp.minimum(least, jnp.min(total))
        most = jnp.maximum(most, jnp.max(total))

    @pl.when(jnp.logical_not((least > LOW) & (most < HIGH)))
    def _():
        def exact(n, carry):
            peak = jnp.full((8, LANES), -1e30, F32)
            for p in range(len(ys)):
                for x, h in ((x1, h1), (x2, h2)):
                    peak = jnp.maximum(peak, fold(scores(p, x, h, n, LANES), jnp.max))
            peak = jnp.max(peak, axis=0, keepdims=True)
            acc = jnp.zeros((8, LANES), F32)
            for p in range(len(ys)):
                for x, h in ((x1, h1), (x2, h2)):
                    acc += fold(jnp.exp(scores(p, x, h, n, LANES) - peak), jnp.sum)
            total = jnp.sum(acc, axis=0, keepdims=True)
            put(n, shift + peak + jnp.log(total))
            return carry

        lax.fori_loop(0, rows // LANES, exact, 0)


def joined(first, second):
    top = jnp.maximum(first, second)
    return top + jnp.log(jnp.exp(first - top) + jnp.exp(second - top))


def own_kernel(xs_ref, y_ref, other_ref, lp_ref, x1, x2, h1, h2):
    spread(xs_ref, x1, x2)

    def put(n, values):
        lp_ref[pl.ds(n, 1), :] = values

    row_sums(x1, x2, (y_ref, other_ref), h1, h2, put)


def more_kernel(x1, x2, y_ref, first_ref, lp_ref, h1, h2):
    def put(n, values):
        values = joined(first_ref[pl.ds(n, 1), :], values)
        for peer in range(lp_ref.shape[0]):
            lp_ref[peer, pl.ds(n, 1), :] = values

    row_sums(x1, x2, (y_ref,), h1, h2, put)


def row_cost(rows, packed):
    return pl.CostEstimate(
        flops=4 * rows * packed * 128, bytes_accessed=2**20, transcendentals=2 * rows * packed
    )


def own_rows(xs, ys, other):
    rows, packed = 2 * xs.shape[0] * 128, 2 * ys.shape[0] * PACKED
    return pl.pallas_call(
        own_kernel,
        out_shape=(
            jax.ShapeDtypeStruct((rows // LANES, LANES), F32),
            jax.ShapeDtypeStruct((rows, LANES), BF16),
            jax.ShapeDtypeStruct((rows, LANES), BF16),
        ),
        scratch_shapes=[pltpu.VMEM((packed, LANES), F32)] * 2,
        name="own_rows",
        compiler_params=params(),
        cost_estimate=row_cost(rows, packed),
    )(xs, ys, other)


def more_rows(x1, x2, ys, first, copies):
    rows, packed = x1.shape[0], ys.shape[0] * PACKED
    return pl.pallas_call(
        more_kernel,
        out_shape=jax.ShapeDtypeStruct((copies, rows // LANES, LANES), F32),
        scratch_shapes=[pltpu.VMEM((packed, LANES), F32)] * 2,
        name="more_rows",
        compiler_params=params(),
        cost_estimate=row_cost(rows, packed),
    )(x1, x2, ys, first)


def log_sum(parts):
    peak = jnp.max(parts, axis=0)
    return peak + jnp.log(jnp.sum(jnp.exp(parts - peak[None]), axis=0))


def weights_kernel(lp_ref, log_a_ref, r_ref, rows_ref, shift_ref):
    line = lax.axis_index("col") // log_a_ref.shape[1] % 2
    masses = jnp.concatenate([log_a_ref[line], log_a_ref[line + 2]], axis=0)
    r = masses - log_sum(lp_ref[...])
    r_ref[...] = r
    shift = jnp.max(r)
    shift_ref[...] = jnp.full(shift_ref.shape, shift)
    for k in range(r.shape[0]):
        rows_ref[pl.ds(k * LANES, LANES), :] = lanes_to_rows(r[k : k + 1] - shift)


def column_sums(x1, x2, rows_ref, shift, ys, owners, lt_ref):
    rows = x1.shape[0]
    chunk = 512

    def scores(x, m, y, chunk):
        at = pl.ds(m * chunk, chunk)
        z = times(x[at, :], y)
        return z + wide(rows_ref[at, :], y.shape[0])

    least, most = jnp.float32(1.0), jnp.float32(1.0)
    for first in range(0, len(ys), 4):
        y = jnp.concatenate([ys[first + k][pl.ds(0, PACKED), :] for k in range(4)], axis=0)
        for side, x in enumerate((x1, x2)):
            acc = jnp.zeros((8, 4 * PACKED), F32)
            for m in range(rows // chunk):
                acc += fold(jnp.exp(scores(x, m, y, chunk)), jnp.sum)
            total = jnp.sum(acc, axis=0, keepdims=True)
            lt = shift + jnp.log(total)
            for k in range(4):
                at = pl.ds(side, 1)
                lt_ref[owners[first + k], at, :] = lt[:, k * PACKED : (k + 1) * PACKED]
            least = jnp.minimum(least, jnp.min(total))
            most = jnp.maximum(most, jnp.max(total))

    @pl.when(jnp.logical_not((least > LOW) & (most < HIGH)))
    def _():
        for p in range(len(ys)):
            y = ys[p][pl.ds(0, PACKED), :]
            for side, x in enumerate((x1, x2)):

                def top(m, peak):
                    return jnp.maximum(peak, fold(scores(x, m, y, 256), jnp.max))

                peak = lax.fori_loop(0, rows // 256, top, jnp.full((8, PACKED), -1e30, F32))
                peak = jnp.max(peak, axis=0, keepdims=True)

                def add(m, acc):
                    return acc + fold(jnp.exp(scores(x, m, y, 256) - peak), jnp.sum)

                acc = lax.fori_loop(0, rows // 256, add, jnp.zeros((8, PACKED), F32))
                total = jnp.sum(acc, axis=0, keepdims=True)
                lt_ref[owners[p], pl.ds(side, 1), :] = shift + peak + jnp.log(total)


def owners_of(count):
    row = lax.axis_index("row")
    chips = count // 2
    chip, core = row // 2, row % 2
    return [
        2 * ((chip + chips - step) % chips) + (core if swap == 0 else 1 - core)
        for swap in range(2)
        for step in range(chips)
    ]


def first_kernel(
    x1, x2, lp_ref, log_a_ref, log_b_ref, sqx_ref, sqy_ref, same, other,
    lt_ref, f_ref, base_ref, rows_ref, shift_ref, r_ref
):
    weights_kernel(lp_ref, log_a_ref, r_ref, rows_ref, shift_ref)
    col, depth = lax.axis_index("col"), r_ref.shape[0] // 2
    at = col // (2 * depth) * depth + col % depth
    f_ref[...] = r_ref[pl.ds(at, 1), :] + 0.5 * sqx_ref[...]
    base_ref[...] = log_b_ref[lax.axis_index("row")] + 0.5 * sqy_ref[...]
    ys = pieces_of((same, other))
    column_sums(x1, x2, rows_ref, shift_ref[:, :1], ys, owners_of(len(ys)), lt_ref)


def second_kernel(x1, x2, rows_ref, shift_ref, same, other, lt_ref):
    ys = pieces_of((same, other))
    column_sums(x1, x2, rows_ref, shift_ref[:, :1], ys, owners_of(len(ys)), lt_ref)


def column_cost(rows, count):
    return pl.CostEstimate(
        flops=4 * rows * count * PACKED * 128,
        bytes_accessed=4 * 2**20,
        transcendentals=2 * rows * count * PACKED,
    )


def first_columns(x1, x2, lps, log_a, log_b, sqx, sqy, same, other):
    rows, count = x1.shape[0], 2 * same.shape[0]
    return pl.pallas_call(
        first_kernel,
        out_shape=(
            jax.ShapeDtypeStruct((count, 2, PACKED), F32),
            jax.ShapeDtypeStruct((1, LANES), F32),
            jax.ShapeDtypeStruct((4, LANES), F32),
            jax.ShapeDtypeStruct((rows, LANES), F32),
            jax.ShapeDtypeStruct((1, LANES), F32),
        ),
        scratch_shapes=[pltpu.VMEM((rows // LANES, LANES), F32)],
        name="first_columns",
        compiler_params=params(),
        cost_estimate=column_cost(rows, count),
    )(x1, x2, lps, log_a, log_b, sqx, sqy, same, other)


def second_columns(x1, x2, weights, shift, same, other):
    rows, count = x1.shape[0], 2 * same.shape[0]
    return pl.pallas_call(
        second_kernel,
        out_shape=jax.ShapeDtypeStruct((count, 2, PACKED), F32),
        name="second_columns",
        compiler_params=params(),
        cost_estimate=column_cost(rows, count),
    )(x1, x2, weights, shift, same, other)


def finish_kernel(lt_ref, base_ref, g_ref):
    g_ref[...] = base_ref[...] - log_sum(lt_ref[...])


def finish(lt, base):
    return pl.pallas_call(
        finish_kernel,
        out_shape=jax.ShapeDtypeStruct((4, LANES), F32),
        name="finish",
        compiler_params=params(),
    )(lt, base)


def exchange(values, axis, groups=None):
    return lax.all_to_all(values, axis, 0, 0, tiled=True, axis_index_groups=groups)


def per_device(source, target, log_a, log_b, start_potential):
    rows, cols = lax.axis_size("row"), lax.axis_size("col")
    chips, half, depth = rows // 2, cols // 2, cols // 4
    xs, ys, sqx, sqy = prepare(source, target, start_potential)

    alike = [[2 * y * depth + k + j for y in range(2) for j in range(depth)] for k in (0, depth)]

    def partner(values):
        return lax.ppermute(values, "col", [(i, i ^ depth) for i in range(cols)])

    def along(values, step):
        pairs = [(2 * x + c, 2 * ((x + step) % chips) + c) for x in range(chips) for c in range(2)]
        return lax.ppermute(values, "row", pairs)

    def swap(values):
        return lax.ppermute(values, "row", [(i, i ^ 1) for i in range(rows)])

    own = jnp.stack([ys] + [along(ys, step) for step in range(1, chips)])
    away = partner(own)
    own_other = swap(own)
    far = lax.ppermute(xs, "col", [(i, (i + half) % cols) for i in range(cols)])
    quarters = [list(range(k, k + depth)) for k in range(0, cols, depth)]
    xs = exchange(pair(xs, far, depth), "col", quarters)
    lp, x1, x2 = own_rows(xs, own, own_other)
    away, lp = lax.optimization_barrier((away, lp))
    away_other = swap(away)
    lp = more_rows(x1, x2, away, lp, 1).reshape(lp.shape)
    lps = more_rows(x1, x2, away_other, lp, half)
    lps = exchange(lps, "col", alike)
    log_a, log_b = log_a.reshape(4, depth, LANES), log_b.reshape(rows, 4, LANES)
    lt_away, f, base, weights, shift = first_columns(
        x1, x2, lps, log_a, log_b, sqx, sqy, away, away_other
    )
    lt_back = partner(lt_away)
    lt = second_columns(x1, x2, weights, shift, own, own_other)
    lt = joined(lt, lt_back)
    lt = exchange(lt, "row").reshape(rows, 4, LANES)
    g = finish(lt, base)
    return f.reshape(LANES), g.reshape(4 * LANES)


def solution(mesh):
    placed = (
        P(("row", "col"), None),
        P(("col", "row"), None),
        P("row"),
        P("col"),
        P(("col", "row")),
    )
    return jax.shard_map(
        per_device,
        mesh=mesh,
        in_specs=placed,
        out_specs=(P(("row", "col")), P(("col", "row"))),
        check_vma=False,
    )
```

```python
import functools

import jax
import jax.numpy as jnp
from jax import lax
from jax.experimental import pallas as pl
from jax.experimental.pallas import tpu as pltpu
from jax.sharding import PartitionSpec as P

F32 = jnp.float32
BF16 = jnp.bfloat16
LANES = 128
PACKED = 256
PIECE = PACKED + 16
LOW, HIGH = 1e-24, 1e36


def params(mib=16):
    return pltpu.CompilerParams(vmem_limit_bytes=mib * 2**20)


def lanes_to_rows(values):
    return jnp.broadcast_to(values, (LANES, LANES)).T


def times(left, right):
    return lax.dot_general(left, right, (((1,), (1,)), ((), ())), preferred_element_type=F32)


def wide(rows, columns):
    return jnp.concatenate([rows] * (columns // LANES), axis=1)


def fold(values, combine):
    rows, columns = values.shape
    return combine(values.reshape(rows // 8, 8, columns), axis=0)


def prepare_kernel(yt_ref, g_ref, ys_ref, part_ref):
    yt = yt_ref[...].astype(F32)
    y = yt.T.astype(BF16)
    ys_ref[pl.ds(0, PACKED), :] = jnp.concatenate([y[:PACKED], y[PACKED:]], axis=1)
    sqy = jnp.sum(yt * yt, axis=0, keepdims=True)
    part_ref[...] = jnp.zeros_like(part_ref)
    for k in range(4):
        own = sqy[:, k * LANES : (k + 1) * LANES]
        rest = g_ref[pl.ds(k, 1), :] - 0.5 * own
        for level in range(3):
            part = rest.astype(BF16).astype(F32)
            part_ref[pl.ds(4 * level + k, 1), :] = part
            rest = rest - part
    ys_ref[pl.ds(PACKED, 16), :] = part_ref[...].astype(BF16)


def prepare(target, g):
    return pl.pallas_call(
        prepare_kernel,
        out_shape=jax.ShapeDtypeStruct((PIECE, LANES), BF16),
        scratch_shapes=[pltpu.VMEM((16, LANES), F32)],
        name="prepare",
        compiler_params=params(),
    )(target.T, g.reshape(4, LANES))


def pair(one, far, peers):
    second = lax.axis_index("col") // (2 * peers) == 1
    both = jnp.stack([jnp.where(second, far, one), jnp.where(second, one, far)])
    return jnp.broadcast_to(both, (peers,) + both.shape)


def spread(xs_ref, x1, x2):
    zeros = jnp.zeros((LANES, 64), BF16)
    peers = xs_ref.shape[0]
    for q in range(2 * peers):
        x = xs_ref[q % peers, q // peers].astype(F32).T.astype(BF16)
        at = pl.ds(q * LANES, LANES)
        x1[at, :] = jnp.concatenate([x, zeros], axis=1)
        x2[at, :] = jnp.concatenate([zeros, x], axis=1)


def pieces_of(refs):
    return [ref.at[k] for ref in refs for k in range(ref.shape[0])]


def row_sums(x1, x2, y_refs, h1, h2, put):
    ys = pieces_of(y_refs)
    rows = x1.shape[0]
    tile = 1024
    terms = []
    for y in ys:
        parts = y[pl.ds(PACKED, 16), :].astype(F32)
        terms.append(parts[0:4] + parts[4:8] + parts[8:12])
    shift = jnp.max(functools.reduce(jnp.maximum, terms))

    def scores(p, x, h, n, columns):
        z = times(ys[p][pl.ds(0, PACKED), :], x[pl.ds(n * columns, columns), :])
        return z + wide(h[pl.ds(p * PACKED, PACKED), :], columns)

    least, most = jnp.float32(1.0), jnp.float32(1.0)
    for n in range(rows // tile):
        acc = jnp.zeros((8, tile), F32)
        for p in range(len(ys)):
            if n == 0:
                term = terms[p] - shift
                for k in range(2):
                    at = pl.ds(p * PACKED + k * LANES, LANES)
                    h1[at, :] = lanes_to_rows(term[k : k + 1])
                    h2[at, :] = lanes_to_rows(term[k + 2 : k + 3])
            for x, h in ((x1, h1), (x2, h2)):
                acc += fold(jnp.exp(scores(p, x, h, n, tile)), jnp.sum)
        total = jnp.sum(acc, axis=0, keepdims=True)
        lp = shift + jnp.log(total)
        for k in range(tile // LANES):
            put(n * (tile // LANES) + k, lp[:, k * LANES : (k + 1) * LANES])
        least = jnp.minimum(least, jnp.min(total))
        most = jnp.maximum(most, jnp.max(total))

    @pl.when(jnp.logical_not((least > LOW) & (most < HIGH)))
    def _():
        def exact(n, carry):
            peak = jnp.full((8, LANES), -1e30, F32)
            for p in range(len(ys)):
                for x, h in ((x1, h1), (x2, h2)):
                    peak = jnp.maximum(peak, fold(scores(p, x, h, n, LANES), jnp.max))
            peak = jnp.max(peak, axis=0, keepdims=True)
            acc = jnp.zeros((8, LANES), F32)
            for p in range(len(ys)):
                for x, h in ((x1, h1), (x2, h2)):
                    acc += fold(jnp.exp(scores(p, x, h, n, LANES) - peak), jnp.sum)
            total = jnp.sum(acc, axis=0, keepdims=True)
            put(n, shift + peak + jnp.log(total))
            return carry

        lax.fori_loop(0, rows // LANES, exact, 0)


def joined(first, second):
    top = jnp.maximum(first, second)
    return top + jnp.log(jnp.exp(first - top) + jnp.exp(second - top))


def own_kernel(xs_ref, y_ref, other_ref, lp_ref, x1, x2, h1, h2):
    spread(xs_ref, x1, x2)

    def put(n, values):
        lp_ref[pl.ds(n, 1), :] = values

    row_sums(x1, x2, (y_ref, other_ref), h1, h2, put)


def more_kernel(x1, x2, y_ref, first_ref, lp_ref, h1, h2):
    def put(n, values):
        values = joined(first_ref[pl.ds(n, 1), :], values)
        for peer in range(lp_ref.shape[0]):
            lp_ref[peer, pl.ds(n, 1), :] = values

    row_sums(x1, x2, (y_ref,), h1, h2, put)


def row_cost(rows, packed):
    return pl.CostEstimate(
        flops=4 * rows * packed * 128, bytes_accessed=2**20, transcendentals=2 * rows * packed
    )


def own_rows(xs, ys, other):
    rows, packed = 2 * xs.shape[0] * 128, 2 * ys.shape[0] * PACKED
    return pl.pallas_call(
        own_kernel,
        out_shape=(
            jax.ShapeDtypeStruct((rows // LANES, LANES), F32),
            jax.ShapeDtypeStruct((rows, LANES), BF16),
            jax.ShapeDtypeStruct((rows, LANES), BF16),
        ),
        scratch_shapes=[pltpu.VMEM((packed, LANES), F32)] * 2,
        name="own_rows",
        compiler_params=params(),
        cost_estimate=row_cost(rows, packed),
    )(xs, ys, other)


def more_rows(x1, x2, ys, first, copies):
    rows, packed = x1.shape[0], ys.shape[0] * PACKED
    return pl.pallas_call(
        more_kernel,
        out_shape=jax.ShapeDtypeStruct((copies, rows // LANES, LANES), F32),
        scratch_shapes=[pltpu.VMEM((packed, LANES), F32)] * 2,
        name="more_rows",
        compiler_params=params(),
        cost_estimate=row_cost(rows, packed),
    )(x1, x2, ys, first)


def log_sum(parts):
    peak = jnp.max(parts, axis=0)
    return peak + jnp.log(jnp.sum(jnp.exp(parts - peak[None]), axis=0))


def weights_kernel(lp_ref, log_a_ref, r_ref, rows_ref, shift_ref):
    line = lax.axis_index("col") // log_a_ref.shape[1] % 2
    masses = jnp.concatenate([log_a_ref[line], log_a_ref[line + 2]], axis=0)
    r = masses - log_sum(lp_ref[...])
    r_ref[...] = r
    shift = jnp.max(r)
    shift_ref[...] = jnp.full(shift_ref.shape, shift)
    for k in range(r.shape[0]):
        rows_ref[pl.ds(k * LANES, LANES), :] = lanes_to_rows(r[k : k + 1] - shift)


def column_sums(x1, x2, rows_ref, shift, ys, owners, lt_ref):
    rows = x1.shape[0]
    chunk = 512

    def scores(x, m, y, chunk):
        at = pl.ds(m * chunk, chunk)
        z = times(x[at, :], y)
        return z + wide(rows_ref[at, :], y.shape[0])

    least, most = jnp.float32(1.0), jnp.float32(1.0)
    for first in range(0, len(ys), 4):
        y = jnp.concatenate([ys[first + k][pl.ds(0, PACKED), :] for k in range(4)], axis=0)
        for side, x in enumerate((x1, x2)):
            acc = jnp.zeros((8, 4 * PACKED), F32)
            for m in range(rows // chunk):
                acc += fold(jnp.exp(scores(x, m, y, chunk)), jnp.sum)
            total = jnp.sum(acc, axis=0, keepdims=True)
            lt = shift + jnp.log(total)
            for k in range(4):
                at = pl.ds(side, 1)
                lt_ref[owners[first + k], at, :] = lt[:, k * PACKED : (k + 1) * PACKED]
            least = jnp.minimum(least, jnp.min(total))
            most = jnp.maximum(most, jnp.max(total))

    @pl.when(jnp.logical_not((least > LOW) & (most < HIGH)))
    def _():
        for p in range(len(ys)):
            y = ys[p][pl.ds(0, PACKED), :]
            for side, x in enumerate((x1, x2)):

                def top(m, peak):
                    return jnp.maximum(peak, fold(scores(x, m, y, 256), jnp.max))

                peak = lax.fori_loop(0, rows // 256, top, jnp.full((8, PACKED), -1e30, F32))
                peak = jnp.max(peak, axis=0, keepdims=True)

                def add(m, acc):
                    return acc + fold(jnp.exp(scores(x, m, y, 256) - peak), jnp.sum)

                acc = lax.fori_loop(0, rows // 256, add, jnp.zeros((8, PACKED), F32))
                total = jnp.sum(acc, axis=0, keepdims=True)
                lt_ref[owners[p], pl.ds(side, 1), :] = shift + peak + jnp.log(total)


def owners_of(count):
    row = lax.axis_index("row")
    chips = count // 2
    chip, core = row // 2, row % 2
    return [
        2 * ((chip + chips - step) % chips) + (core if swap == 0 else 1 - core)
        for swap in range(2)
        for step in range(chips)
    ]


def first_kernel(x1, x2, lp_ref, log_a_ref, same, other, lt_ref, r_ref, rows_ref, shift_ref):
    weights_kernel(lp_ref, log_a_ref, r_ref, rows_ref, shift_ref)
    ys = pieces_of((same, other))
    column_sums(x1, x2, rows_ref, shift_ref[:, :1], ys, owners_of(len(ys)), lt_ref)


def second_kernel(
    x1, x2, rows_ref, shift_ref, r_ref, same, other, log_b_ref, lt_ref, f_ref, base_ref
):
    ys = pieces_of((same, other))
    column_sums(x1, x2, rows_ref, shift_ref[:, :1], ys, owners_of(len(ys)), lt_ref)
    col, depth = lax.axis_index("col"), r_ref.shape[0] // 2
    at = col // (2 * depth) * depth + col % depth
    x = x1[pl.ds(pl.multiple_of(at * LANES, LANES), LANES), :].astype(F32).T
    f_ref[...] = r_ref[pl.ds(at, 1), :] + 0.5 * jnp.sum(x * x, axis=0, keepdims=True)
    y = same[0, pl.ds(0, PACKED), :].astype(F32).T
    log_b = log_b_ref[lax.axis_index("row")]
    for side in range(2):
        part = y[64 * side : 64 * (side + 1)]
        sq = jnp.sum(part * part, axis=0, keepdims=True)
        for k in range(2):
            row = 2 * side + k
            base_ref[pl.ds(row, 1), :] = (
                log_b[row : row + 1] + 0.5 * sq[:, k * LANES : (k + 1) * LANES]
            )


def column_cost(rows, count):
    return pl.CostEstimate(
        flops=4 * rows * count * PACKED * 128,
        bytes_accessed=4 * 2**20,
        transcendentals=2 * rows * count * PACKED,
    )


def first_columns(x1, x2, lps, log_a, same, other):
    rows, count = x1.shape[0], 2 * same.shape[0]
    return pl.pallas_call(
        first_kernel,
        out_shape=(
            jax.ShapeDtypeStruct((count, 2, PACKED), F32),
            jax.ShapeDtypeStruct((rows // LANES, LANES), F32),
            jax.ShapeDtypeStruct((rows, LANES), F32),
            jax.ShapeDtypeStruct((1, LANES), F32),
        ),
        name="first_columns",
        compiler_params=params(),
        cost_estimate=column_cost(rows, count),
    )(x1, x2, lps, log_a, same, other)


def second_columns(x1, x2, weights, shift, r, same, other, log_b):
    rows, count = x1.shape[0], 2 * same.shape[0]
    return pl.pallas_call(
        second_kernel,
        out_shape=(
            jax.ShapeDtypeStruct((count, 2, PACKED), F32),
            jax.ShapeDtypeStruct((1, LANES), F32),
            jax.ShapeDtypeStruct((4, LANES), F32),
        ),
        name="second_columns",
        compiler_params=params(),
        cost_estimate=column_cost(rows, count),
    )(x1, x2, weights, shift, r, same, other, log_b)


def finish_kernel(lt_ref, base_ref, own_ref, g_ref, f_ref):
    g_ref[...] = base_ref[...] - log_sum(lt_ref[...])
    f_ref[...] = own_ref[...]


def finish(lt, base, own):
    return pl.pallas_call(
        finish_kernel,
        out_shape=(
            jax.ShapeDtypeStruct((4, LANES), F32),
            jax.ShapeDtypeStruct((1, LANES), F32),
        ),
        name="finish",
        compiler_params=params(),
    )(lt, base, own)


def exchange(values, axis, groups=None):
    return lax.all_to_all(values, axis, 0, 0, tiled=True, axis_index_groups=groups)


def per_device(source, target, log_a, log_b, start_potential):
    rows, cols = lax.axis_size("row"), lax.axis_size("col")
    chips, half, depth = rows // 2, cols // 2, cols // 4
    one, ys = source.T, prepare(target, start_potential)

    alike = [[2 * y * depth + k + j for y in range(2) for j in range(depth)] for k in (0, depth)]

    def partner(values):
        return lax.ppermute(values, "col", [(i, i ^ depth) for i in range(cols)])

    def along(values, step):
        pairs = [(2 * x + c, 2 * ((x + step) % chips) + c) for x in range(chips) for c in range(2)]
        return lax.ppermute(values, "row", pairs)

    def swap(values):
        return lax.ppermute(values, "row", [(i, i ^ 1) for i in range(rows)])

    own = jnp.stack([ys] + [along(ys, step) for step in range(1, chips)])
    away = partner(own)
    own_other = swap(own)
    far = lax.ppermute(one, "col", [(i, (i + half) % cols) for i in range(cols)])
    quarters = [list(range(k, k + depth)) for k in range(0, cols, depth)]
    xs = exchange(pair(one, far, depth), "col", quarters)
    lp, x1, x2 = own_rows(xs, own, own_other)
    away, lp = lax.optimization_barrier((away, lp))
    away_other = swap(away)
    lp = more_rows(x1, x2, away, lp, 1).reshape(lp.shape)
    lps = more_rows(x1, x2, away_other, lp, half)
    lps = exchange(lps, "col", alike)
    log_a, log_b = log_a.reshape(4, depth, LANES), log_b.reshape(rows, 4, LANES)
    lt_away, r, weights, shift = first_columns(x1, x2, lps, log_a, away, away_other)
    lt_back = partner(lt_away)
    lt, f, base = second_columns(x1, x2, weights, shift, r, own, own_other, log_b)
    lt = joined(lt, lt_back)
    lt = exchange(lt, "row").reshape(rows, 4, LANES)
    g, f = finish(lt, base, f)
    return f.reshape(LANES), g.reshape(4 * LANES)


def solution(mesh):
    placed = (
        P(("row", "col"), None),
        P(("col", "row"), None),
        P("row"),
        P("col"),
        P(("col", "row")),
    )
    return jax.shard_map(
        per_device,
        mesh=mesh,
        in_specs=placed,
        out_specs=(P(("row", "col")), P(("col", "row"))),
        check_vma=False,
    )
```

```python
import functools

import jax
import jax.numpy as jnp
from jax import lax
from jax.experimental import pallas as pl
from jax.experimental.pallas import tpu as pltpu
from jax.sharding import PartitionSpec as P

F32 = jnp.float32
BF16 = jnp.bfloat16
LANES = 128
PACKED = 256
PIECE = PACKED + 16
LOW, HIGH = 1e-24, 1e36


def params(mib=16):
    return pltpu.CompilerParams(vmem_limit_bytes=mib * 2**20)


def lanes_to_rows(values):
    return jnp.broadcast_to(values, (LANES, LANES)).T


def times(left, right):
    return lax.dot_general(left, right, (((1,), (1,)), ((), ())), preferred_element_type=F32)


def wide(rows, columns):
    return jnp.concatenate([rows] * (columns // LANES), axis=1)


def fold(values, combine):
    rows, columns = values.shape
    return combine(values.reshape(rows // 8, 8, columns), axis=0)


def prepare_kernel(yt_ref, g_ref, xt_ref, ys_ref, one_ref, part_ref):
    one_ref[...] = xt_ref[...]
    yt = yt_ref[...].astype(F32)
    y = yt.T.astype(BF16)
    ys_ref[pl.ds(0, PACKED), :] = jnp.concatenate([y[:PACKED], y[PACKED:]], axis=1)
    sqy = jnp.sum(yt * yt, axis=0, keepdims=True)
    part_ref[...] = jnp.zeros_like(part_ref)
    for k in range(4):
        own = sqy[:, k * LANES : (k + 1) * LANES]
        rest = g_ref[pl.ds(k, 1), :] - 0.5 * own
        for level in range(3):
            part = rest.astype(BF16).astype(F32)
            part_ref[pl.ds(4 * level + k, 1), :] = part
            rest = rest - part
    ys_ref[pl.ds(PACKED, 16), :] = part_ref[...].astype(BF16)


def prepare(target, g, xt):
    return pl.pallas_call(
        prepare_kernel,
        out_shape=(
            jax.ShapeDtypeStruct((PIECE, LANES), BF16),
            jax.ShapeDtypeStruct(xt.shape, BF16),
        ),
        scratch_shapes=[pltpu.VMEM((16, LANES), F32)],
        name="prepare",
        compiler_params=params(),
    )(target.T, g.reshape(4, LANES), xt)


def spread(xs_ref, x1, x2):
    zeros = jnp.zeros((LANES, 64), BF16)
    peers = xs_ref.shape[0]
    half = lax.axis_index("col") // (2 * peers)
    for q in range(2 * peers):
        side = half if q < peers else 1 - half
        x = xs_ref[q % peers, side].astype(F32).T.astype(BF16)
        at = pl.ds(q * LANES, LANES)
        x1[at, :] = jnp.concatenate([x, zeros], axis=1)
        x2[at, :] = jnp.concatenate([zeros, x], axis=1)


def pieces_of(refs):
    return [ref.at[k] for ref in refs for k in range(ref.shape[0])]


def spread_terms(ys, h1, h2):
    terms = []
    for y in ys:
        parts = y[pl.ds(PACKED, 16), :].astype(F32)
        terms.append(parts[0:4] + parts[4:8] + parts[8:12])
    shift = jnp.max(functools.reduce(jnp.maximum, terms))
    for p, term in enumerate(terms):
        term = term - shift
        for k in range(2):
            at = pl.ds(p * PACKED + k * LANES, LANES)
            h1[at, :] = lanes_to_rows(term[k : k + 1])
            h2[at, :] = lanes_to_rows(term[k + 2 : k + 3])
    return shift


def terms_kernel(y_ref, other_ref, h1, h2, shift_ref):
    shift = spread_terms(pieces_of((y_ref, other_ref)), h1, h2)
    shift_ref[...] = jnp.full(shift_ref.shape, shift)


def target_terms(ys, other):
    packed = 2 * ys.shape[0] * PACKED
    return pl.pallas_call(
        terms_kernel,
        out_shape=(
            jax.ShapeDtypeStruct((packed, LANES), F32),
            jax.ShapeDtypeStruct((packed, LANES), F32),
            jax.ShapeDtypeStruct((1, LANES), F32),
        ),
        name="target_terms",
        compiler_params=params(),
    )(ys, other)


def row_sums(x1, x2, y_refs, h1, h2, shift, put):
    ys = pieces_of(y_refs)
    rows = x1.shape[0]
    tile = 1024

    def scores(p, x, h, n, columns):
        z = times(ys[p][pl.ds(0, PACKED), :], x[pl.ds(n * columns, columns), :])
        return z + wide(h[pl.ds(p * PACKED, PACKED), :], columns)

    least, most = jnp.float32(1.0), jnp.float32(1.0)
    for n in range(rows // tile):
        acc = jnp.zeros((8, tile), F32)
        for p in range(len(ys)):
            for x, h in ((x1, h1), (x2, h2)):
                acc += fold(jnp.exp(scores(p, x, h, n, tile)), jnp.sum)
        total = jnp.sum(acc, axis=0, keepdims=True)
        lp = shift + jnp.log(total)
        for k in range(tile // LANES):
            put(n * (tile // LANES) + k, lp[:, k * LANES : (k + 1) * LANES])
        least = jnp.minimum(least, jnp.min(total))
        most = jnp.maximum(most, jnp.max(total))

    @pl.when(jnp.logical_not((least > LOW) & (most < HIGH)))
    def _():
        def exact(n, carry):
            peak = jnp.full((8, LANES), -1e30, F32)
            for p in range(len(ys)):
                for x, h in ((x1, h1), (x2, h2)):
                    peak = jnp.maximum(peak, fold(scores(p, x, h, n, LANES), jnp.max))
            peak = jnp.max(peak, axis=0, keepdims=True)
            acc = jnp.zeros((8, LANES), F32)
            for p in range(len(ys)):
                for x, h in ((x1, h1), (x2, h2)):
                    acc += fold(jnp.exp(scores(p, x, h, n, LANES) - peak), jnp.sum)
            total = jnp.sum(acc, axis=0, keepdims=True)
            put(n, shift + peak + jnp.log(total))
            return carry

        lax.fori_loop(0, rows // LANES, exact, 0)


def joined(first, second):
    top = jnp.maximum(first, second)
    return top + jnp.log(jnp.exp(first - top) + jnp.exp(second - top))


def own_kernel(xs_ref, y_ref, other_ref, h1, h2, shift_ref, lp_ref, x1, x2):
    spread(xs_ref, x1, x2)

    def put(n, values):
        lp_ref[pl.ds(n, 1), :] = values

    row_sums(x1, x2, (y_ref, other_ref), h1, h2, shift_ref[:, :1], put)


def more_kernel(x1, x2, y_ref, first_ref, lp_ref, h1, h2):
    def put(n, values):
        values = joined(first_ref[pl.ds(n, 1), :], values)
        for peer in range(lp_ref.shape[0]):
            lp_ref[peer, pl.ds(n, 1), :] = values

    shift = spread_terms(pieces_of((y_ref,)), h1, h2)
    row_sums(x1, x2, (y_ref,), h1, h2, shift, put)


def row_cost(rows, packed):
    return pl.CostEstimate(
        flops=4 * rows * packed * 128, bytes_accessed=2**20, transcendentals=2 * rows * packed
    )


def own_rows(xs, ys, other, h1, h2, shift):
    rows, packed = 2 * xs.shape[0] * 128, 2 * ys.shape[0] * PACKED
    return pl.pallas_call(
        own_kernel,
        out_shape=(
            jax.ShapeDtypeStruct((rows // LANES, LANES), F32),
            jax.ShapeDtypeStruct((rows, LANES), BF16),
            jax.ShapeDtypeStruct((rows, LANES), BF16),
        ),
        name="own_rows",
        compiler_params=params(),
        cost_estimate=row_cost(rows, packed),
    )(xs, ys, other, h1, h2, shift)


def more_rows(x1, x2, ys, first, copies):
    rows, packed = x1.shape[0], ys.shape[0] * PACKED
    return pl.pallas_call(
        more_kernel,
        out_shape=jax.ShapeDtypeStruct((copies, rows // LANES, LANES), F32),
        scratch_shapes=[pltpu.VMEM((packed, LANES), F32)] * 2,
        name="more_rows",
        compiler_params=params(),
        cost_estimate=row_cost(rows, packed),
    )(x1, x2, ys, first)


def log_sum(parts):
    peak = jnp.max(parts, axis=0)
    return peak + jnp.log(jnp.sum(jnp.exp(parts - peak[None]), axis=0))


def weights_kernel(lp_ref, log_a_ref, r_ref, rows_ref, shift_ref):
    line = lax.axis_index("col") // log_a_ref.shape[1] % 2
    masses = jnp.concatenate([log_a_ref[line], log_a_ref[line + 2]], axis=0)
    r = masses - log_sum(lp_ref[...])
    r_ref[...] = r
    shift = jnp.max(r)
    shift_ref[...] = jnp.full(shift_ref.shape, shift)
    for k in range(r.shape[0]):
        rows_ref[pl.ds(k * LANES, LANES), :] = lanes_to_rows(r[k : k + 1] - shift)


def column_sums(x1, x2, rows_ref, shift, ys, owners, lt_ref):
    rows = x1.shape[0]
    chunk = 512

    def scores(x, m, y, chunk):
        at = pl.ds(m * chunk, chunk)
        z = times(x[at, :], y)
        return z + wide(rows_ref[at, :], y.shape[0])

    least, most = jnp.float32(1.0), jnp.float32(1.0)
    for first in range(0, len(ys), 4):
        y = jnp.concatenate([ys[first + k][pl.ds(0, PACKED), :] for k in range(4)], axis=0)
        for side, x in enumerate((x1, x2)):
            acc = jnp.zeros((8, 4 * PACKED), F32)
            for m in range(rows // chunk):
                acc += fold(jnp.exp(scores(x, m, y, chunk)), jnp.sum)
            total = jnp.sum(acc, axis=0, keepdims=True)
            lt = shift + jnp.log(total)
            for k in range(4):
                at = pl.ds(side, 1)
                lt_ref[owners[first + k], at, :] = lt[:, k * PACKED : (k + 1) * PACKED]
            least = jnp.minimum(least, jnp.min(total))
            most = jnp.maximum(most, jnp.max(total))

    @pl.when(jnp.logical_not((least > LOW) & (most < HIGH)))
    def _():
        for p in range(len(ys)):
            y = ys[p][pl.ds(0, PACKED), :]
            for side, x in enumerate((x1, x2)):

                def top(m, peak):
                    return jnp.maximum(peak, fold(scores(x, m, y, 256), jnp.max))

                peak = lax.fori_loop(0, rows // 256, top, jnp.full((8, PACKED), -1e30, F32))
                peak = jnp.max(peak, axis=0, keepdims=True)

                def add(m, acc):
                    return acc + fold(jnp.exp(scores(x, m, y, 256) - peak), jnp.sum)

                acc = lax.fori_loop(0, rows // 256, add, jnp.zeros((8, PACKED), F32))
                total = jnp.sum(acc, axis=0, keepdims=True)
                lt_ref[owners[p], pl.ds(side, 1), :] = shift + peak + jnp.log(total)


def owners_of(count):
    row = lax.axis_index("row")
    chips = count // 2
    chip, core = row // 2, row % 2
    return [
        2 * ((chip + chips - step) % chips) + (core if swap == 0 else 1 - core)
        for swap in range(2)
        for step in range(chips)
    ]


def first_kernel(x1, x2, lp_ref, log_a_ref, same, other, lt_ref, r_ref, rows_ref, shift_ref):
    weights_kernel(lp_ref, log_a_ref, r_ref, rows_ref, shift_ref)
    ys = pieces_of((same, other))
    column_sums(x1, x2, rows_ref, shift_ref[:, :1], ys, owners_of(len(ys)), lt_ref)


def second_kernel(
    x1, x2, rows_ref, shift_ref, r_ref, same, other, log_b_ref, lt_ref, f_ref, base_ref
):
    ys = pieces_of((same, other))
    column_sums(x1, x2, rows_ref, shift_ref[:, :1], ys, owners_of(len(ys)), lt_ref)
    col, depth = lax.axis_index("col"), r_ref.shape[0] // 2
    at = col // (2 * depth) * depth + col % depth
    x = x1[pl.ds(pl.multiple_of(at * LANES, LANES), LANES), :].astype(F32).T
    f_ref[...] = r_ref[pl.ds(at, 1), :] + 0.5 * jnp.sum(x * x, axis=0, keepdims=True)
    y = same[0, pl.ds(0, PACKED), :].astype(F32).T
    log_b = log_b_ref[lax.axis_index("row")]
    for side in range(2):
        part = y[64 * side : 64 * (side + 1)]
        sq = jnp.sum(part * part, axis=0, keepdims=True)
        for k in range(2):
            row = 2 * side + k
            base_ref[pl.ds(row, 1), :] = (
                log_b[row : row + 1] + 0.5 * sq[:, k * LANES : (k + 1) * LANES]
            )


def column_cost(rows, count):
    return pl.CostEstimate(
        flops=4 * rows * count * PACKED * 128,
        bytes_accessed=4 * 2**20,
        transcendentals=2 * rows * count * PACKED,
    )


def first_columns(x1, x2, lps, log_a, same, other):
    rows, count = x1.shape[0], 2 * same.shape[0]
    return pl.pallas_call(
        first_kernel,
        out_shape=(
            jax.ShapeDtypeStruct((count, 2, PACKED), F32),
            jax.ShapeDtypeStruct((rows // LANES, LANES), F32),
            jax.ShapeDtypeStruct((rows, LANES), F32),
            jax.ShapeDtypeStruct((1, LANES), F32),
        ),
        name="first_columns",
        compiler_params=params(),
        cost_estimate=column_cost(rows, count),
    )(x1, x2, lps, log_a, same, other)


def second_columns(x1, x2, weights, shift, r, same, other, log_b):
    rows, count = x1.shape[0], 2 * same.shape[0]
    return pl.pallas_call(
        second_kernel,
        out_shape=(
            jax.ShapeDtypeStruct((count, 2, PACKED), F32),
            jax.ShapeDtypeStruct((1, LANES), F32),
            jax.ShapeDtypeStruct((4, LANES), F32),
        ),
        name="second_columns",
        compiler_params=params(),
        cost_estimate=column_cost(rows, count),
    )(x1, x2, weights, shift, r, same, other, log_b)


def finish_kernel(lt_ref, base_ref, own_ref, g_ref, f_ref):
    g_ref[...] = base_ref[...] - log_sum(lt_ref[...])
    f_ref[...] = own_ref[...]


def finish(lt, base, own):
    return pl.pallas_call(
        finish_kernel,
        out_shape=(
            jax.ShapeDtypeStruct((4, LANES), F32),
            jax.ShapeDtypeStruct((1, LANES), F32),
        ),
        name="finish",
        compiler_params=params(),
    )(lt, base, own)


def exchange(values, axis, groups=None):
    return lax.all_to_all(values, axis, 0, 0, tiled=True, axis_index_groups=groups)


def per_device(source, target, log_a, log_b, start_potential):
    rows, cols = lax.axis_size("row"), lax.axis_size("col")
    chips, half, depth = rows // 2, cols // 2, cols // 4
    ys, one = prepare(target, start_potential, source.T)

    alike = [[2 * y * depth + k + j for y in range(2) for j in range(depth)] for k in (0, depth)]

    def partner(values):
        return lax.ppermute(values, "col", [(i, i ^ depth) for i in range(cols)])

    def along(values, step):
        pairs = [(2 * x + c, 2 * ((x + step) % chips) + c) for x in range(chips) for c in range(2)]
        return lax.ppermute(values, "row", pairs)

    def swap(values):
        return lax.ppermute(values, "row", [(i, i ^ 1) for i in range(rows)])

    own = jnp.stack([ys] + [along(ys, step) for step in range(1, chips)])
    away = partner(own)
    own_other = swap(own)
    far = lax.ppermute(source.T, "col", [(i, (i + half) % cols) for i in range(cols)])
    quarters = [list(range(k, k + depth)) for k in range(0, cols, depth)]
    both = jnp.stack([one, far])
    xs = exchange(jnp.broadcast_to(both, (depth,) + both.shape), "col", quarters)
    lp, x1, x2 = own_rows(xs, own, own_other, *target_terms(own, own_other))
    away, lp = lax.optimization_barrier((away, lp))
    away_other = swap(away)
    lp = more_rows(x1, x2, away, lp, 1).reshape(lp.shape)
    lps = more_rows(x1, x2, away_other, lp, half)
    lps = exchange(lps, "col", alike)
    log_a, log_b = log_a.reshape(4, depth, LANES), log_b.reshape(rows, 4, LANES)
    lt_away, r, weights, shift = first_columns(x1, x2, lps, log_a, away, away_other)
    lt_back = partner(lt_away)
    lt, f, base = second_columns(x1, x2, weights, shift, r, own, own_other, log_b)
    lt = joined(lt, lt_back)
    lt = exchange(lt, "row").reshape(rows, 4, LANES)
    g, f = finish(lt, base, f)
    return f.reshape(LANES), g.reshape(4 * LANES)


def solution(mesh):
    placed = (
        P(("row", "col"), None),
        P(("col", "row"), None),
        P("row"),
        P("col"),
        P(("col", "row")),
    )
    return jax.shard_map(
        per_device,
        mesh=mesh,
        in_specs=placed,
        out_specs=(P(("row", "col")), P(("col", "row"))),
        check_vma=False,
    )
```

```python
import functools

import jax
import jax.numpy as jnp
from jax import lax
from jax.experimental import pallas as pl
from jax.experimental.pallas import tpu as pltpu
from jax.sharding import PartitionSpec as P

F32 = jnp.float32
BF16 = jnp.bfloat16
LANES = 128
PACKED = 256
PIECE = PACKED + 16
LOW, HIGH = 1e-24, 1e36


def params(mib=16):
    return pltpu.CompilerParams(vmem_limit_bytes=mib * 2**20)


def lanes_to_rows(values):
    return jnp.broadcast_to(values, (LANES, LANES)).T


def times(left, right):
    return lax.dot_general(left, right, (((1,), (1,)), ((), ())), preferred_element_type=F32)


def wide(rows, columns):
    return jnp.concatenate([rows] * (columns // LANES), axis=1)


def fold(values, combine):
    rows, columns = values.shape
    return combine(values.reshape(rows // 8, 8, columns), axis=0)


def prepare_kernel(yt_ref, g_ref, xt_ref, ys_ref, one_ref, part_ref):
    one_ref[...] = xt_ref[...]
    yt = yt_ref[...].astype(F32)
    y = yt.T.astype(BF16)
    ys_ref[pl.ds(0, PACKED), :] = jnp.concatenate([y[:PACKED], y[PACKED:]], axis=1)
    sqy = jnp.sum(yt * yt, axis=0, keepdims=True)
    part_ref[...] = jnp.zeros_like(part_ref)
    for k in range(4):
        own = sqy[:, k * LANES : (k + 1) * LANES]
        rest = g_ref[pl.ds(k, 1), :] - 0.5 * own
        for level in range(3):
            part = rest.astype(BF16).astype(F32)
            part_ref[pl.ds(4 * level + k, 1), :] = part
            rest = rest - part
    ys_ref[pl.ds(PACKED, 16), :] = part_ref[...].astype(BF16)


def prepare(target, g, xt):
    return pl.pallas_call(
        prepare_kernel,
        out_shape=(
            jax.ShapeDtypeStruct((PIECE, LANES), BF16),
            jax.ShapeDtypeStruct(xt.shape, BF16),
        ),
        scratch_shapes=[pltpu.VMEM((16, LANES), F32)],
        name="prepare",
        compiler_params=params(),
    )(target.T, g.reshape(4, LANES), xt)


def spread(xs_ref, x1, x2):
    zeros = jnp.zeros((LANES, 64), BF16)
    peers = xs_ref.shape[0]
    half = lax.axis_index("col") // (2 * peers)
    for q in range(2 * peers):
        side = half if q < peers else 1 - half
        x = xs_ref[q % peers, side].astype(F32).T.astype(BF16)
        at = pl.ds(q * LANES, LANES)
        x1[at, :] = jnp.concatenate([x, zeros], axis=1)
        x2[at, :] = jnp.concatenate([zeros, x], axis=1)


def pieces_of(refs):
    return [ref.at[k] for ref in refs for k in range(ref.shape[0])]


def spread_terms(ys, h1, h2):
    terms = []
    for y in ys:
        parts = y[pl.ds(PACKED, 16), :].astype(F32)
        terms.append(parts[0:4] + parts[4:8] + parts[8:12])
    shift = jnp.max(functools.reduce(jnp.maximum, terms))
    for p, term in enumerate(terms):
        term = term - shift
        for k in range(2):
            at = pl.ds(p * PACKED + k * LANES, LANES)
            h1[at, :] = lanes_to_rows(term[k : k + 1])
            h2[at, :] = lanes_to_rows(term[k + 2 : k + 3])
    return shift


def terms_kernel(same, other_ref, log_b_ref, h1, h2, shift_ref, base_ref):
    y_ref = same
    shift = spread_terms(pieces_of((y_ref, other_ref)), h1, h2)
    shift_ref[...] = jnp.full(shift_ref.shape, shift)
    y = same[0, pl.ds(0, PACKED), :].astype(F32).T
    log_b = log_b_ref[lax.axis_index("row")]
    for side in range(2):
        part = y[64 * side : 64 * (side + 1)]
        sq = jnp.sum(part * part, axis=0, keepdims=True)
        for k in range(2):
            row = 2 * side + k
            base_ref[pl.ds(row, 1), :] = (
                log_b[row : row + 1] + 0.5 * sq[:, k * LANES : (k + 1) * LANES]
            )


def target_terms(ys, other, log_b):
    packed = 2 * ys.shape[0] * PACKED
    return pl.pallas_call(
        terms_kernel,
        out_shape=(
            jax.ShapeDtypeStruct((packed, LANES), F32),
            jax.ShapeDtypeStruct((packed, LANES), F32),
            jax.ShapeDtypeStruct((1, LANES), F32),
            jax.ShapeDtypeStruct((4, LANES), F32),
        ),
        name="target_terms",
        compiler_params=params(),
    )(ys, other, log_b)


def row_sums(x1, x2, y_refs, h1, h2, shift, put):
    ys = pieces_of(y_refs)
    rows = x1.shape[0]
    tile = 1024

    def scores(p, x, h, n, columns):
        z = times(ys[p][pl.ds(0, PACKED), :], x[pl.ds(n * columns, columns), :])
        return z + wide(h[pl.ds(p * PACKED, PACKED), :], columns)

    least, most = jnp.float32(1.0), jnp.float32(1.0)
    for n in range(rows // tile):
        acc = jnp.zeros((8, tile), F32)
        for p in range(len(ys)):
            for x, h in ((x1, h1), (x2, h2)):
                acc += fold(jnp.exp(scores(p, x, h, n, tile)), jnp.sum)
        total = jnp.sum(acc, axis=0, keepdims=True)
        lp = shift + jnp.log(total)
        for k in range(tile // LANES):
            put(n * (tile // LANES) + k, lp[:, k * LANES : (k + 1) * LANES])
        least = jnp.minimum(least, jnp.min(total))
        most = jnp.maximum(most, jnp.max(total))

    @pl.when(jnp.logical_not((least > LOW) & (most < HIGH)))
    def _():
        def exact(n, carry):
            peak = jnp.full((8, LANES), -1e30, F32)
            for p in range(len(ys)):
                for x, h in ((x1, h1), (x2, h2)):
                    peak = jnp.maximum(peak, fold(scores(p, x, h, n, LANES), jnp.max))
            peak = jnp.max(peak, axis=0, keepdims=True)
            acc = jnp.zeros((8, LANES), F32)
            for p in range(len(ys)):
                for x, h in ((x1, h1), (x2, h2)):
                    acc += fold(jnp.exp(scores(p, x, h, n, LANES) - peak), jnp.sum)
            total = jnp.sum(acc, axis=0, keepdims=True)
            put(n, shift + peak + jnp.log(total))
            return carry

        lax.fori_loop(0, rows // LANES, exact, 0)


def joined(first, second):
    top = jnp.maximum(first, second)
    return top + jnp.log(jnp.exp(first - top) + jnp.exp(second - top))


def own_kernel(xs_ref, y_ref, other_ref, h1, h2, shift_ref, lp_ref, x1, x2):
    spread(xs_ref, x1, x2)

    def put(n, values):
        lp_ref[pl.ds(n, 1), :] = values

    row_sums(x1, x2, (y_ref, other_ref), h1, h2, shift_ref[:, :1], put)


def more_kernel(x1, x2, y_ref, first_ref, lp_ref, h1, h2):
    def put(n, values):
        values = joined(first_ref[pl.ds(n, 1), :], values)
        for peer in range(lp_ref.shape[0]):
            lp_ref[peer, pl.ds(n, 1), :] = values

    shift = spread_terms(pieces_of((y_ref,)), h1, h2)
    row_sums(x1, x2, (y_ref,), h1, h2, shift, put)


def row_cost(rows, packed):
    return pl.CostEstimate(
        flops=4 * rows * packed * 128, bytes_accessed=2**20, transcendentals=2 * rows * packed
    )


def own_rows(xs, ys, other, h1, h2, shift):
    rows, packed = 2 * xs.shape[0] * 128, 2 * ys.shape[0] * PACKED
    return pl.pallas_call(
        own_kernel,
        out_shape=(
            jax.ShapeDtypeStruct((rows // LANES, LANES), F32),
            jax.ShapeDtypeStruct((rows, LANES), BF16),
            jax.ShapeDtypeStruct((rows, LANES), BF16),
        ),
        name="own_rows",
        compiler_params=params(),
        cost_estimate=row_cost(rows, packed),
    )(xs, ys, other, h1, h2, shift)


def more_rows(x1, x2, ys, first, copies):
    rows, packed = x1.shape[0], ys.shape[0] * PACKED
    return pl.pallas_call(
        more_kernel,
        out_shape=jax.ShapeDtypeStruct((copies, rows // LANES, LANES), F32),
        scratch_shapes=[pltpu.VMEM((packed, LANES), F32)] * 2,
        name="more_rows",
        compiler_params=params(),
        cost_estimate=row_cost(rows, packed),
    )(x1, x2, ys, first)


def log_sum(parts):
    peak = jnp.max(parts, axis=0)
    return peak + jnp.log(jnp.sum(jnp.exp(parts - peak[None]), axis=0))


def weights_kernel(lp_ref, log_a_ref, r_ref, rows_ref, shift_ref):
    line = lax.axis_index("col") // log_a_ref.shape[1] % 2
    masses = jnp.concatenate([log_a_ref[line], log_a_ref[line + 2]], axis=0)
    r = masses - log_sum(lp_ref[...])
    r_ref[...] = r
    shift = jnp.max(r)
    shift_ref[...] = jnp.full(shift_ref.shape, shift)
    for k in range(r.shape[0]):
        rows_ref[pl.ds(k * LANES, LANES), :] = lanes_to_rows(r[k : k + 1] - shift)


def column_sums(x1, x2, rows_ref, shift, ys, owners, lt_ref):
    rows = x1.shape[0]
    chunk = 512

    def scores(x, m, y, chunk):
        at = pl.ds(m * chunk, chunk)
        z = times(x[at, :], y)
        return z + wide(rows_ref[at, :], y.shape[0])

    least, most = jnp.float32(1.0), jnp.float32(1.0)
    for first in range(0, len(ys), 4):
        y = jnp.concatenate([ys[first + k][pl.ds(0, PACKED), :] for k in range(4)], axis=0)
        for side, x in enumerate((x1, x2)):
            acc = jnp.zeros((8, 4 * PACKED), F32)
            for m in range(rows // chunk):
                acc += fold(jnp.exp(scores(x, m, y, chunk)), jnp.sum)
            total = jnp.sum(acc, axis=0, keepdims=True)
            lt = shift + jnp.log(total)
            for k in range(4):
                at = pl.ds(side, 1)
                lt_ref[owners[first + k], at, :] = lt[:, k * PACKED : (k + 1) * PACKED]
            least = jnp.minimum(least, jnp.min(total))
            most = jnp.maximum(most, jnp.max(total))

    @pl.when(jnp.logical_not((least > LOW) & (most < HIGH)))
    def _():
        for p in range(len(ys)):
            y = ys[p][pl.ds(0, PACKED), :]
            for side, x in enumerate((x1, x2)):

                def top(m, peak):
                    return jnp.maximum(peak, fold(scores(x, m, y, 256), jnp.max))

                peak = lax.fori_loop(0, rows // 256, top, jnp.full((8, PACKED), -1e30, F32))
                peak = jnp.max(peak, axis=0, keepdims=True)

                def add(m, acc):
                    return acc + fold(jnp.exp(scores(x, m, y, 256) - peak), jnp.sum)

                acc = lax.fori_loop(0, rows // 256, add, jnp.zeros((8, PACKED), F32))
                total = jnp.sum(acc, axis=0, keepdims=True)
                lt_ref[owners[p], pl.ds(side, 1), :] = shift + peak + jnp.log(total)


def owners_of(count):
    row = lax.axis_index("row")
    chips = count // 2
    chip, core = row // 2, row % 2
    return [
        2 * ((chip + chips - step) % chips) + (core if swap == 0 else 1 - core)
        for swap in range(2)
        for step in range(chips)
    ]


def first_kernel(x1, x2, lp_ref, log_a_ref, same, other, lt_ref, r_ref, rows_ref, shift_ref):
    weights_kernel(lp_ref, log_a_ref, r_ref, rows_ref, shift_ref)
    ys = pieces_of((same, other))
    column_sums(x1, x2, rows_ref, shift_ref[:, :1], ys, owners_of(len(ys)), lt_ref)


def second_kernel(
    x1, x2, rows_ref, shift_ref, r_ref, same, other, lt_ref, f_ref
):
    ys = pieces_of((same, other))
    column_sums(x1, x2, rows_ref, shift_ref[:, :1], ys, owners_of(len(ys)), lt_ref)
    col, depth = lax.axis_index("col"), r_ref.shape[0] // 2
    at = col // (2 * depth) * depth + col % depth
    x = x1[pl.ds(pl.multiple_of(at * LANES, LANES), LANES), :].astype(F32).T
    f_ref[...] = r_ref[pl.ds(at, 1), :] + 0.5 * jnp.sum(x * x, axis=0, keepdims=True)


def column_cost(rows, count):
    return pl.CostEstimate(
        flops=4 * rows * count * PACKED * 128,
        bytes_accessed=4 * 2**20,
        transcendentals=2 * rows * count * PACKED,
    )


def first_columns(x1, x2, lps, log_a, same, other):
    rows, count = x1.shape[0], 2 * same.shape[0]
    return pl.pallas_call(
        first_kernel,
        out_shape=(
            jax.ShapeDtypeStruct((count, 2, PACKED), F32),
            jax.ShapeDtypeStruct((rows // LANES, LANES), F32),
            jax.ShapeDtypeStruct((rows, LANES), F32),
            jax.ShapeDtypeStruct((1, LANES), F32),
        ),
        name="first_columns",
        compiler_params=params(),
        cost_estimate=column_cost(rows, count),
    )(x1, x2, lps, log_a, same, other)


def second_columns(x1, x2, weights, shift, r, same, other):
    rows, count = x1.shape[0], 2 * same.shape[0]
    return pl.pallas_call(
        second_kernel,
        out_shape=(
            jax.ShapeDtypeStruct((count, 2, PACKED), F32),
            jax.ShapeDtypeStruct((1, LANES), F32),
        ),
        name="second_columns",
        compiler_params=params(),
        cost_estimate=column_cost(rows, count),
    )(x1, x2, weights, shift, r, same, other)


def finish_kernel(lt_ref, base_ref, own_ref, g_ref, f_ref):
    g_ref[...] = base_ref[...] - log_sum(lt_ref[...])
    f_ref[...] = own_ref[...]


def finish(lt, base, own):
    return pl.pallas_call(
        finish_kernel,
        out_shape=(
            jax.ShapeDtypeStruct((4, LANES), F32),
            jax.ShapeDtypeStruct((1, LANES), F32),
        ),
        name="finish",
        compiler_params=params(),
    )(lt, base, own)


def exchange(values, axis, groups=None):
    return lax.all_to_all(values, axis, 0, 0, tiled=True, axis_index_groups=groups)


def per_device(source, target, log_a, log_b, start_potential):
    rows, cols = lax.axis_size("row"), lax.axis_size("col")
    chips, half, depth = rows // 2, cols // 2, cols // 4
    ys, one = prepare(target, start_potential, source.T)

    alike = [[2 * y * depth + k + j for y in range(2) for j in range(depth)] for k in (0, depth)]

    def partner(values):
        return lax.ppermute(values, "col", [(i, i ^ depth) for i in range(cols)])

    def along(values, step):
        pairs = [(2 * x + c, 2 * ((x + step) % chips) + c) for x in range(chips) for c in range(2)]
        return lax.ppermute(values, "row", pairs)

    def swap(values):
        return lax.ppermute(values, "row", [(i, i ^ 1) for i in range(rows)])

    own = jnp.stack([ys] + [along(ys, step) for step in range(1, chips)])
    away = partner(own)
    own_other = swap(own)
    far = lax.ppermute(source.T, "col", [(i, (i + half) % cols) for i in range(cols)])
    quarters = [list(range(k, k + depth)) for k in range(0, cols, depth)]
    both = jnp.stack([one, far])
    xs = exchange(jnp.broadcast_to(both, (depth,) + both.shape), "col", quarters)
    log_b = log_b.reshape(rows, 4, LANES)
    *terms, base = target_terms(own, own_other, log_b)
    lp, x1, x2 = own_rows(xs, own, own_other, *terms)
    away, lp = lax.optimization_barrier((away, lp))
    away_other = swap(away)
    lp = more_rows(x1, x2, away, lp, 1).reshape(lp.shape)
    lps = more_rows(x1, x2, away_other, lp, half)
    lps = exchange(lps, "col", alike)
    log_a = log_a.reshape(4, depth, LANES)
    lt_away, r, weights, shift = first_columns(x1, x2, lps, log_a, away, away_other)
    lt_back = partner(lt_away)
    lt, f = second_columns(x1, x2, weights, shift, r, own, own_other)
    lt = joined(lt, lt_back)
    lt = exchange(lt, "row").reshape(rows, 4, LANES)
    g, f = finish(lt, base, f)
    return f.reshape(LANES), g.reshape(4 * LANES)


def solution(mesh):
    placed = (
        P(("row", "col"), None),
        P(("col", "row"), None),
        P("row"),
        P("col"),
        P(("col", "row")),
    )
    return jax.shard_map(
        per_device,
        mesh=mesh,
        in_specs=placed,
        out_specs=(P(("row", "col")), P(("col", "row"))),
        check_vma=False,
    )
```
